512 devices in a mesh: rows: 32 (over x, z), feat: 16 (over y, core).
Axes of the slice: x: 4, y: 8, z: 8, core: 2. Of those that a mesh axis runs over, the one named last changes fastest.
Arguments:
- block_values: bfloat16 [32, 16, 12, 128, 128], P('rows', 'feat'), may hold values from -6 to 6
- block_rows: int32 [32, 16, 12], P('rows', 'feat'), may hold values from 0 to 3, as said below
- block_cols: int32 [32, 16, 12], P('rows', 'feat'), may hold values from 0 to 3, as said below
- test_matrix: bfloat16 [8192, 256], P('feat'), may hold values from -18 to 18
Outputs:
- doc_basis: float32 [16384, 256], P(('rows', 'feat'))
The draws below stay inside these ranges and needn't reach their ends.
Inputs may be any that keep to these rules, and one draw needn't show every extreme that they name: Within one tile the 12 pairs (block_rows, block_cols) are distinct, and every block row and every block column of the tile occurs among them. `block_cols`: see block_rows: paired entry by entry with it.
All inputs are finite; a program needn't handle non-finite values.
Results may differ from the reference program's by a relative error of at most 0.0034.
Values may be sent and summed in bfloat16 or wider, within the bound.
No kernel may reach another device: no remote copies, remote signals or barrier semaphores. Data moves between devices by JAX's collectives and lax.ppermute only.
A program may use at most 64 MiB of HBM per device.

```python
import jax
import jax.numpy as jnp
from jax import lax

BLK = 128
RANK = 256
TILE_GRID_SIDE = 4
NONZERO_BLOCKS = 12
SLABS = 32
STRIPS = 16
DOCS = 16384
FEATS = 8192


def picked_cells(key):
    total = SLABS * STRIPS

    def one_tile(tile_key):
        first, second = jax.random.split(tile_key)
        sorted_index = jax.random.permutation(first, TILE_GRID_SIDE * TILE_GRID_SIDE).astype(jnp.int32)
        singular_values = jax.random.permutation(second, TILE_GRID_SIDE).astype(jnp.int32)
        cell_ids = jnp.arange(TILE_GRID_SIDE * TILE_GRID_SIDE, dtype=jnp.int32)
        block_row_lookup = cell_ids // TILE_GRID_SIDE
        block_column_lookup = cell_ids % TILE_GRID_SIDE
        extra_weight = (block_column_lookup == singular_values[block_row_lookup]).astype(jnp.int32) * (TILE_GRID_SIDE * TILE_GRID_SIDE)
        unused_value, selected_blocks = lax.top_k(extra_weight + sorted_index, NONZERO_BLOCKS)
        return selected_blocks.astype(jnp.int32)
    keys = jax.random.split(jax.random.fold_in(key, 7), total)
    return jax.vmap(one_tile)(keys).reshape(SLABS, STRIPS, NONZERO_BLOCKS)


def shared_uniform(key):
    return jax.random.uniform(jax.random.fold_in(key, 101), (BLK,), jnp.float32, 0.0, 1.0)


def draw_block_rows(key, part):
    return picked_cells(key) // TILE_GRID_SIDE


def draw_block_cols(key, part):
    return picked_cells(key) % TILE_GRID_SIDE


def draw_block_values(key, part):
    base = shared_uniform(key)
    key = jax.random.fold_in(key, 11)
    noise_key, sign_key = jax.random.split(key)
    shape = (SLABS, STRIPS, NONZERO_BLOCKS, BLK, BLK)
    coins = jax.random.bernoulli(sign_key, 0.5, (SLABS, STRIPS, NONZERO_BLOCKS, BLK, 1))
    signs = jnp.where(coins, 1.0, -1.0).astype(jnp.float32)
    noise = jax.random.truncated_normal(noise_key, -4.0, 4.0, shape, jnp.float32)
    pattern = 1.41421356 * lax.erf_inv(2.0 * jnp.clip(base, 0.0015, 0.9985) - 1.0)
    return (noise + 0.42 * signs * pattern).astype(jnp.bfloat16)


def draw_test_matrix(key, part):
    base = shared_uniform(key)
    key = jax.random.fold_in(key, 13)
    noise_key, coef_key = jax.random.split(key)
    noise = jax.random.truncated_normal(noise_key, -4.0, 4.0, (FEATS, RANK), jnp.float32)
    coefs = jax.random.truncated_normal(coef_key, -3.0, 3.0, (FEATS // BLK, RANK), jnp.float32)
    pattern = 1.41421356 * lax.erf_inv(2.0 * jnp.clip(base, 0.0015, 0.9985) - 1.0)
    pattern_full = jnp.tile(pattern, FEATS // BLK)
    coef_full = jnp.repeat(coefs, BLK, axis=0)
    return (noise + 1.5 * pattern_full[:, None] * coef_full).astype(jnp.bfloat16)


def setup_inputs(seed: int = 0) -> dict:
    key_of = jax.random.split(jax.random.key(seed), 5)
    return {
        "block_values": draw_block_values(jax.random.fold_in(key_of[4], 71), 0),
        "block_rows": draw_block_rows(jax.random.fold_in(key_of[4], 71), 0),
        "block_cols": draw_block_cols(jax.random.fold_in(key_of[4], 71), 0),
        "test_matrix": draw_test_matrix(jax.random.fold_in(key_of[4], 71), 0),
    }


def tile_rows(values, rows_idx, cols_idx, basis):
    count = basis.shape[0] // BLK
    pieces = basis.reshape(count, BLK, basis.shape[1])[cols_idx]
    prod = jnp.einsum('nij,njr->nir', values.astype(jnp.float32), pieces.astype(jnp.float32), precision=lax.Precision.HIGHEST)
    onehot = (rows_idx[None, :] == jnp.arange(count)[:, None]).astype(jnp.float32)
    summed = jnp.einsum('kn,nir->kir', onehot, prod, precision=lax.Precision.HIGHEST)
    return summed.reshape(count * BLK, basis.shape[1])

def tile_cols(values, rows_idx, cols_idx, basis):
    count = basis.shape[0] // BLK
    pieces = basis.reshape(count, BLK, basis.shape[1])[rows_idx]
    prod = jnp.einsum('nij,nir->njr', values.astype(jnp.float32), pieces.astype(jnp.float32), precision=lax.Precision.HIGHEST)
    onehot = (cols_idx[None, :] == jnp.arange(count)[:, None]).astype(jnp.float32)
    summed = jnp.einsum('kn,nir->kir', onehot, prod, precision=lax.Precision.HIGHEST)
    return summed.reshape(count * BLK, basis.shape[1])

def whiten(matrix):
    gram = jnp.einsum('dr,ds->rs', matrix, matrix, precision=lax.Precision.HIGHEST)
    lower = jnp.linalg.cholesky(gram)
    identity = jnp.eye(gram.shape[0], dtype=gram.dtype)
    inverse = lax.linalg.triangular_solve(lower, identity, left_side=True, lower=True)
    return jnp.dot(matrix, inverse.T, precision=lax.Precision.HIGHEST)

def apply_slab(block_values, block_rows, block_cols, basis):
    strips = basis.reshape(STRIPS, TILE_GRID_SIDE * BLK, basis.shape[1])

    def per_slab(items):
        parts = jax.vmap(tile_rows)(items[0], items[1], items[2], strips)
        return lax.optimization_barrier(jnp.sum(parts, axis=0))
    out = lax.map(per_slab, (block_values, block_rows, block_cols))
    return out.reshape(DOCS, basis.shape[1])

def apply_transpose(block_values, block_rows, block_cols, basis):
    slabs = basis.reshape(SLABS, TILE_GRID_SIDE * BLK, basis.shape[1])

    def per_strip(items):
        parts = jax.vmap(tile_cols)(items[0], items[1], items[2], slabs)
        return lax.optimization_barrier(jnp.sum(parts, axis=0))
    out = lax.map(per_strip, (jnp.swapaxes(block_values, 0, 1), jnp.swapaxes(block_rows, 0, 1), jnp.swapaxes(block_cols, 0, 1)))
    return out.reshape(FEATS, basis.shape[1])

def reference(block_values, block_rows, block_cols, test_matrix):
    sketch = apply_slab(block_values, block_rows, block_cols, test_matrix)
    basis = whiten(sketch).astype(jnp.bfloat16)
    cosketch = apply_transpose(block_values, block_rows, block_cols, basis)
    cobasis = cosketch.astype(jnp.bfloat16)
    resketch = apply_slab(block_values, block_rows, block_cols, cobasis)
    return whiten(resketch) * jnp.sqrt(jnp.float32(DOCS))
```

```python
import jax
import jax.numpy as jnp
from jax import lax
from jax.experimental import pallas as pl
from jax.experimental.pallas import tpu as pltpu
from jax.sharding import PartitionSpec as P

HIGHEST = lax.Precision.HIGHEST
VMEM = pl.BlockSpec(memory_space=pltpu.VMEM)
SMEM = pl.BlockSpec(memory_space=pltpu.SMEM)


def dot(a, b, precision=None):
    return jnp.dot(a, b, preferred_element_type=jnp.float32, precision=precision)


def dot_t(a, b, precision=None):
    dims = (((0,), (0,)), ((), ()))
    return lax.dot_general(a, b, dims, preferred_element_type=jnp.float32, precision=precision)


def first_kernel(rows_ref, cols_ref, values_ref, test_ref, tile_ref, part_ref):
    count, width = values_ref.shape[0], values_ref.shape[1]
    tile_ref[...] = jnp.zeros_like(tile_ref)
    for n in range(count):
        row = pl.multiple_of(rows_ref[n] * width, width)
        col = pl.multiple_of(cols_ref[n] * width, width)
        tile_ref[pl.ds(row, width), pl.ds(col, width)] = values_ref[n]
    part_ref[...] = dot(tile_ref[...], test_ref[...]).reshape(part_ref.shape)


def second_kernel(tile_ref, sketch_ref, out_ref):
    sketch = sketch_ref[...]
    tile = tile_ref[...]
    groups = out_ref.shape[0]
    rank = sketch.shape[1]
    high = sketch.astype(jnp.bfloat16)
    rest = sketch - high.astype(jnp.float32)
    mid = rest.astype(jnp.bfloat16)
    low = (rest - mid.astype(jnp.float32)).astype(jnp.bfloat16)
    co = dot_t(tile, high) + (dot_t(tile, mid) + dot_t(tile, low))
    split = tile.shape[1] // groups
    out_ref[:, :split, :] = co.reshape(groups, split, rank)
    gram = dot_t(sketch, sketch, HIGHEST)
    out_ref[:, split:, :] = gram.reshape(groups, rank // groups, rank)


def inverse_factor(gram):
    lower = jnp.linalg.cholesky(gram)
    identity = jnp.eye(gram.shape[0], dtype=gram.dtype)
    return lax.linalg.triangular_solve(lower, identity, left_side=True, lower=True)


def to_each(x, axis):
    return lax.all_to_all(x, axis, 0, 0, tiled=True)


def from_each(x, axis):
    size = lax.axis_size(axis)
    return to_each(jnp.broadcast_to(x[None], (size,) + x.shape), axis)


def per_device(block_values, block_rows, block_cols, test_matrix):
    values = block_values[0, 0]
    side, rank = test_matrix.shape
    n_rows, n_feat = lax.axis_size("rows"), lax.axis_size("feat")
    scale = jnp.sqrt(jnp.float32(side * n_rows))
    share = side // n_feat
    split = side // n_rows

    tile, part = pl.pallas_call(
        first_kernel,
        in_specs=[SMEM, SMEM, VMEM, VMEM],
        out_specs=[VMEM, VMEM],
        out_shape=[
            jax.ShapeDtypeStruct((side, side), jnp.bfloat16),
            jax.ShapeDtypeStruct((n_feat, share, rank), jnp.float32),
        ],
    )(block_rows[0, 0], block_cols[0, 0], values, test_matrix)
    sketch = lax.all_gather(jnp.sum(to_each(part, "feat"), axis=0), "feat", axis=0, tiled=True)

    both = pl.pallas_call(
        second_kernel,
        in_specs=[VMEM, VMEM],
        out_specs=VMEM,
        out_shape=jax.ShapeDtypeStruct((n_rows, split + rank // n_rows, rank), jnp.float32),
    )(tile, sketch)
    both = from_each(jnp.sum(to_each(both, "rows"), axis=0), "rows")
    cosketch = both[:, :split].reshape(side, rank)
    inverse = inverse_factor(both[:, split:].reshape(rank, rank))
    cobasis = jnp.dot(cosketch, inverse.T, precision=HIGHEST).astype(jnp.bfloat16)

    part = dot(tile, cobasis).reshape(n_feat, share, rank)
    resketch = jnp.sum(to_each(part, "feat"), axis=0)
    gram = dot_t(resketch, resketch, HIGHEST).reshape(n_rows, rank // n_rows, rank)
    gram = jnp.sum(to_each(gram, "rows"), axis=0)
    gram = jnp.sum(lax.all_gather(gram, "feat", axis=0), axis=0)
    gram = from_each(gram, "rows").reshape(rank, rank)
    return jnp.dot(resketch, inverse_factor(gram).T, precision=HIGHEST) * scale


def solution(mesh):
    placed = (
        P("rows", "feat", None, None, None),
        P("rows", "feat", None),
        P("rows", "feat", None),
        P("feat", None),
    )
    return jax.shard_map(
        per_device, mesh=mesh, in_specs=placed, out_specs=P(("rows", "feat"), None), check_vma=False
    )
```

```python
import jax
import jax.numpy as jnp
from jax import lax
from jax.experimental import pallas as pl
from jax.experimental.pallas import tpu as pltpu
from jax.sharding import PartitionSpec as P

HIGHEST = lax.Precision.HIGHEST
VMEM = pl.BlockSpec(memory_space=pltpu.VMEM)
SMEM = pl.BlockSpec(memory_space=pltpu.SMEM)
SUB = 8


def dot(a, b, precision=None, contract=(1, 0)):
    dims = (((contract[0],), (contract[1],)), ((), ()))
    return lax.dot_general(a, b, dims, preferred_element_type=jnp.float32, precision=precision)


def terms(x):
    high = x.astype(jnp.bfloat16)
    rest = x - high.astype(jnp.float32)
    mid = rest.astype(jnp.bfloat16)
    return high, mid, (rest - mid.astype(jnp.float32)).astype(jnp.bfloat16)


def dot_terms(tile, x, contract=(1, 0)):
    high, mid, low = terms(x)
    small = dot(tile, mid, contract=contract) + dot(tile, low, contract=contract)
    return dot(tile, high, contract=contract) + small


def block_inverse(block):
    n = block.shape[0]
    shape = (SUB, n)
    parts = [block[i : i + SUB] for i in range(0, n, SUB)]
    lane = lax.broadcasted_iota(jnp.int32, shape, 1)
    sub = lax.broadcasted_iota(jnp.int32, shape, 0)
    full = lambda v: jnp.broadcast_to(v, shape)
    done = []
    for j in range(n // SUB):
        b = parts[j]
        base = j * SUB
        cols = [full(b[:, base + k : base + k + 1]) for k in range(SUB)]
        final = jnp.zeros(shape, jnp.float32)
        for k in range(SUB):
            pivot = full(cols[k][k : k + 1, :])
            inv = 1.0 / pivot
            root = lax.rsqrt(pivot)
            here = lane == base + k
            own = sub == k
            m = cols[k] * inv
            row = full(b[k : k + 1, :])
            past = jnp.where(lane < base + k, row * root, 0.0)
            final = jnp.where(own, jnp.where(here, root, past), final)
            for q in range(k + 1, SUB):
                c = full(cols[q][k : k + 1, :])
                cols[q] = jnp.where(own, c * inv, cols[q] - m * c)
            one = jnp.where(here, 1.0, row)
            b = jnp.where(own, one * inv, jnp.where(here, 0.0, b) - m * one)
        done.append(final)
        rows = [full(b[k : k + 1, :]) for k in range(SUB)]
        inside = (lane >= base) & (lane < base + SUB)
        for i in range(j + 1, n // SUB):
            t = [full(parts[i][:, base + k : base + k + 1]) * rows[k] for k in range(SUB)]
            t = ((t[0] + t[1]) + (t[2] + t[3])) + ((t[4] + t[5]) + (t[6] + t[7]))
            parts[i] = jnp.where(inside, 0.0, parts[i]) - t
    return jnp.concatenate(done, axis=0)


def inverse_factor(gram):
    n = gram.shape[0]
    half = n // 2
    r = lax.broadcasted_iota(jnp.int32, (n, n), 0)
    c = lax.broadcasted_iota(jnp.int32, (n, n), 1)
    diag = jnp.where(r == c, gram, 0.0)
    across = lax.rsqrt(jnp.sum(diag, axis=0, keepdims=True))
    down = lax.rsqrt(jnp.sum(diag, axis=1, keepdims=True))
    unit = jnp.where(r == c, 1.0, gram * across * down)
    first = block_inverse(unit[:half, :half])
    lower = dot(unit[half:, :half], first, HIGHEST, (1, 1))
    second = block_inverse(unit[half:, half:] - dot(lower, lower, HIGHEST, (1, 1)))
    corner = -dot(second, dot(lower, first, HIGHEST), HIGHEST)
    top = jnp.concatenate([first, jnp.zeros_like(first)], axis=1)
    return jnp.concatenate([top, jnp.concatenate([corner, second], axis=1)], axis=0) * across


def sketch_kernel(rows_ref, cols_ref, values_ref, test_ref, tile_ref, part_ref):
    count, width = values_ref.shape[0], values_ref.shape[1]
    tile_ref[...] = jnp.zeros_like(tile_ref)
    for n in range(count):
        row = pl.multiple_of(rows_ref[n] * width, width)
        col = pl.multiple_of(cols_ref[n] * width, width)
        tile_ref[pl.ds(row, width), pl.ds(col, width)] = values_ref[n]
    part_ref[...] = dot(tile_ref[...], test_ref[...]).reshape(part_ref.shape)


def cosketch_kernel(side_ref, tile_ref, sketch_ref, out_ref):
    sketch = sketch_ref[...]
    groups, _, half = out_ref.shape
    co = dot_terms(tile_ref[...], sketch, (0, 0))
    split = co.shape[0] // groups
    out_ref[:, :split, :] = co[:, :half].reshape(groups, split, half)
    out_ref[:, split : 2 * split, :] = co[:, half:].reshape(groups, split, half)
    chosen = jnp.where(side_ref[0] == 0, sketch[:, :half], sketch[:, half:])
    gram = dot(sketch, chosen, HIGHEST, (0, 0))
    out_ref[:, 2 * split :, :] = gram.reshape(groups, gram.shape[0] // groups, half)


def resketch_kernel(tile_ref, both_ref, part_ref, gram_ref):
    both = both_ref[...]
    side = tile_ref.shape[0]
    split = side // both.shape[0]
    left = both[:, :split, :].reshape(side, both.shape[2])
    right = both[:, split : 2 * split, :].reshape(side, both.shape[2])
    co = jnp.concatenate([left, right], axis=1)
    part_ref[...] = dot_terms(tile_ref[...], co).reshape(part_ref.shape)
    gram_ref[...] = both[:, 2 * split :, :].reshape(gram_ref.shape)


def factor_kernel(side_ref, own_ref, other_ref, out_ref):
    own, other = own_ref[...], other_ref[...]
    left = jnp.where(side_ref[0] == 0, own, other)
    right = jnp.where(side_ref[0] == 0, other, own)
    out_ref[...] = inverse_factor(jnp.concatenate([left, right], axis=1))


def gram_kernel(parts_ref, inverse_ref, share_ref, gram_ref):
    share = dot(jnp.sum(parts_ref[...], axis=0), inverse_ref[...], HIGHEST, (1, 1))
    share_ref[...] = share
    gram_ref[...] = dot(share, share, HIGHEST, (0, 0)).reshape(gram_ref.shape)


def final_kernel(scale, share_ref, gram_ref, out_ref):
    rank = out_ref.shape[1]
    inverse = inverse_factor(gram_ref[...].reshape(rank, rank))
    out_ref[...] = dot(share_ref[...], inverse, HIGHEST, (1, 1)) * scale


def to_each(x, axis):
    return lax.all_to_all(x, axis, 0, 0, tiled=True)


def from_each(x, axis):
    size = lax.axis_size(axis)
    return to_each(jnp.broadcast_to(x[None], (size,) + x.shape), axis)


def f32(*shape):
    return jax.ShapeDtypeStruct(shape, jnp.float32)


def per_device(block_values, block_rows, block_cols, test_matrix):
    values = block_values[0, 0]
    side, rank = test_matrix.shape
    half = rank // 2
    n_rows, n_feat = lax.axis_size("rows"), lax.axis_size("feat")
    scale = float(side * n_rows) ** 0.5
    share = side // n_feat
    core = (lax.axis_index("feat") % 2).astype(jnp.int32).reshape(1)

    tile, part = pl.pallas_call(
        sketch_kernel,
        in_specs=[SMEM, SMEM, VMEM, VMEM],
        out_specs=[VMEM, VMEM],
        out_shape=[jax.ShapeDtypeStruct((side, side), jnp.bfloat16), f32(n_feat, share, rank)],
    )(block_rows[0, 0], block_cols[0, 0], values, test_matrix)
    sketch = lax.all_gather(jnp.sum(to_each(part, "feat"), axis=0), "feat", axis=0, tiled=True)

    both = pl.pallas_call(
        cosketch_kernel,
        in_specs=[SMEM, VMEM, VMEM],
        out_specs=VMEM,
        out_shape=f32(n_rows, 2 * side // n_rows + rank // n_rows, half),
    )(core, tile, sketch)
    both = from_each(jnp.sum(to_each(both, "rows"), axis=0), "rows")

    part, own = pl.pallas_call(
        resketch_kernel,
        in_specs=[VMEM, VMEM],
        out_specs=[VMEM, VMEM],
        out_shape=[f32(n_feat, share, rank), f32(rank, half)],
    )(tile, both)
    parts = to_each(part, "feat")
    other = lax.ppermute(own, "feat", [(i, i ^ 1) for i in range(n_feat)])
    inverse = pl.pallas_call(
        factor_kernel,
        in_specs=[SMEM, VMEM, VMEM],
        out_specs=VMEM,
        out_shape=f32(rank, rank),
        cost_estimate=pl.CostEstimate(flops=10**10, bytes_accessed=10**6, transcendentals=0),
    )(core, own, other)

    resketch, gram = pl.pallas_call(
        gram_kernel,
        in_specs=[VMEM, VMEM],
        out_specs=[VMEM, VMEM],
        out_shape=[f32(share, rank), f32(n_rows, rank // n_rows, rank)],
    )(parts, inverse)
    gram = jnp.sum(to_each(gram, "rows"), axis=0)
    gram = jnp.sum(lax.all_gather(gram, "feat", axis=0), axis=0)
    return pl.pallas_call(
        lambda *refs: final_kernel(scale, *refs),
        in_specs=[VMEM, VMEM],
        out_specs=VMEM,
        out_shape=f32(share, rank),
    )(resketch, from_each(gram, "rows"))


def solution(mesh):
    placed = (
        P("rows", "feat", None, None, None),
        P("rows", "feat", None),
        P("rows", "feat", None),
        P("feat", None),
    )
    return jax.shard_map(
        per_device, mesh=mesh, in_specs=placed, out_specs=P(("rows", "feat"), None), check_vma=False
    )
```

```python
import jax
import jax.numpy as jnp
from jax import lax
from jax.experimental import pallas as pl
from jax.experimental.pallas import tpu as pltpu
from jax.sharding import PartitionSpec as P

HIGHEST = lax.Precision.HIGHEST
PARAMS = pltpu.CompilerParams(vmem_limit_bytes=12 * 2**20)
VMEM = pl.BlockSpec(memory_space=pltpu.VMEM)
SMEM = pl.BlockSpec(memory_space=pltpu.SMEM)
SUB = 8


def dot(a, b, precision=None, contract=(1, 0)):
    dims = (((contract[0],), (contract[1],)), ((), ()))
    return lax.dot_general(a, b, dims, preferred_element_type=jnp.float32, precision=precision)


def terms(x):
    high = x.astype(jnp.bfloat16)
    rest = x - high.astype(jnp.float32)
    mid = rest.astype(jnp.bfloat16)
    return high, mid, (rest - mid.astype(jnp.float32)).astype(jnp.bfloat16)


def dot_terms(tile, x, contract=(1, 0)):
    high, mid, low = terms(x)
    small = dot(tile, mid, contract=contract) + dot(tile, low, contract=contract)
    return dot(tile, high, contract=contract) + small


def block_inverse(block):
    n = block.shape[0]
    shape = (SUB, n)
    parts = [block[i : i + SUB] for i in range(0, n, SUB)]
    lane = lax.broadcasted_iota(jnp.int32, shape, 1)
    sub = lax.broadcasted_iota(jnp.int32, shape, 0)
    full = lambda v: jnp.broadcast_to(v, shape)
    done = []
    for j in range(n // SUB):
        rows = parts[j]
        base = j * SUB
        cols = [full(rows[:, base + k : base + k + 1]) for k in range(SUB)]
        final = jnp.zeros(shape, jnp.float32)
        for k in range(0, SUB, 2):
            a = full(cols[k][k : k + 1, :])
            b = full(cols[k + 1][k : k + 1, :])
            d = full(cols[k + 1][k + 1 : k + 2, :])
            det = a * d - b * b
            inv = 1.0 / det
            first, second = sub == k, sub == k + 1
            own = first | second
            m1 = jnp.where(first, -1.0, jnp.where(second, 0.0, cols[k]))
            m2 = jnp.where(second, -1.0, jnp.where(first, 0.0, cols[k + 1]))
            w1 = m1 * d - m2 * b
            w2 = m2 * a - m1 * b
            for q in range(k + 2, SUB):
                z = w1 * full(cols[q][k : k + 1, :]) + w2 * full(cols[q][k + 1 : k + 2, :])
                cols[q] = jnp.where(own, 0.0, cols[q]) - z * inv
            here, after = lane == base + k, lane == base + k + 1
            r1 = jnp.where(here, 1.0, jnp.where(after, 0.0, full(rows[k : k + 1, :])))
            r2 = jnp.where(after, 1.0, jnp.where(here, 0.0, full(rows[k + 1 : k + 2, :])))
            root = lax.rsqrt(a)
            inv_a = root * root
            u1 = jnp.where(lane <= base + k, r1 * root, 0.0)
            u2 = (r2 - (b * inv_a) * r1) * lax.rsqrt(det * inv_a)
            u2 = jnp.where(lane <= base + k + 1, u2, 0.0)
            final = jnp.where(first, u1, jnp.where(second, u2, final))
            rows = jnp.where(own | here | after, 0.0, rows) - (w1 * r1 + w2 * r2) * inv
        done.append(final)
        pivots = [full(rows[k : k + 1, :]) for k in range(SUB)]
        inside = (lane >= base) & (lane < base + SUB)
        for i in range(j + 1, n // SUB):
            t = [full(parts[i][:, base + k : base + k + 1]) * pivots[k] for k in range(SUB)]
            t = ((t[0] + t[1]) + (t[2] + t[3])) + ((t[4] + t[5]) + (t[6] + t[7]))
            parts[i] = jnp.where(inside, 0.0, parts[i]) - t
    return jnp.concatenate(done, axis=0)


def inverse_factor(gram):
    n = gram.shape[0]
    half = n // 2
    r = lax.broadcasted_iota(jnp.int32, (n, n), 0)
    c = lax.broadcasted_iota(jnp.int32, (n, n), 1)
    diag = jnp.where(r == c, gram, 0.0)
    across = lax.rsqrt(jnp.sum(diag, axis=0, keepdims=True))
    down = lax.rsqrt(jnp.sum(diag, axis=1, keepdims=True))
    unit = jnp.where(r == c, 1.0, gram * across * down)
    first = block_inverse(unit[:half, :half])
    lower = dot(unit[half:, :half], first, HIGHEST, (1, 1))
    second = block_inverse(unit[half:, half:] - dot(lower, lower, HIGHEST, (1, 1)))
    corner = -dot(second, dot(lower, first, HIGHEST), HIGHEST)
    top = jnp.concatenate([first, jnp.zeros_like(first)], axis=1)
    return jnp.concatenate([top, jnp.concatenate([corner, second], axis=1)], axis=0) * across


def sketch_kernel(rows_ref, cols_ref, values_ref, test_ref, tile_ref, part_ref):
    count, width = values_ref.shape[0], values_ref.shape[1]
    tile_ref[...] = jnp.zeros_like(tile_ref)
    for n in range(count):
        row = pl.multiple_of(rows_ref[n] * width, width)
        col = pl.multiple_of(cols_ref[n] * width, width)
        tile_ref[pl.ds(row, width), pl.ds(col, width)] = values_ref[n]
    part_ref[...] = dot(tile_ref[...], test_ref[...]).reshape(part_ref.shape)


def cosketch_kernel(side_ref, tile_ref, sketch_ref, out_ref):
    sketch = sketch_ref[...]
    groups, _, half = out_ref.shape
    co = dot_terms(tile_ref[...], sketch, (0, 0))
    split = co.shape[0] // groups
    out_ref[:, :split, :] = co[:, :half].reshape(groups, split, half)
    out_ref[:, split : 2 * split, :] = co[:, half:].reshape(groups, split, half)
    chosen = jnp.where(side_ref[0] == 0, sketch[:, :half], sketch[:, half:])
    gram = dot(sketch, chosen, HIGHEST, (0, 0))
    out_ref[:, 2 * split :, :] = gram.reshape(groups, gram.shape[0] // groups, half)


def resketch_kernel(tile_ref, both_ref, part_ref, gram_ref):
    both = both_ref[...]
    side = tile_ref.shape[0]
    split = side // both.shape[0]
    left = both[:, :split, :].reshape(side, both.shape[2])
    right = both[:, split : 2 * split, :].reshape(side, both.shape[2])
    co = jnp.concatenate([left, right], axis=1)
    part_ref[...] = dot_terms(tile_ref[...], co).reshape(part_ref.shape)
    gram_ref[...] = both[:, 2 * split :, :].reshape(gram_ref.shape)


def factor_kernel(side_ref, own_ref, other_ref, out_ref):
    own, other = own_ref[...], other_ref[...]
    left = jnp.where(side_ref[0] == 0, own, other)
    right = jnp.where(side_ref[0] == 0, other, own)
    out_ref[...] = inverse_factor(jnp.concatenate([left, right], axis=1))


def gram_kernel(parts_ref, inverse_ref, share_ref, gram_ref):
    share = dot(jnp.sum(parts_ref[...], axis=0), inverse_ref[...], HIGHEST, (1, 1))
    share_ref[...] = share
    gram_ref[...] = dot(share, share, HIGHEST, (0, 0)).reshape(gram_ref.shape)


def final_kernel(scale, share_ref, gram_ref, out_ref):
    rank = out_ref.shape[1]
    inverse = inverse_factor(gram_ref[...].reshape(rank, rank))
    out_ref[...] = dot(share_ref[...], inverse, HIGHEST, (1, 1)) * scale


def to_each(x, axis):
    return lax.all_to_all(x, axis, 0, 0, tiled=True)


def from_each(x, axis):
    size = lax.axis_size(axis)
    return to_each(jnp.broadcast_to(x[None], (size,) + x.shape), axis)


def f32(*shape):
    return jax.ShapeDtypeStruct(shape, jnp.float32)


def per_device(block_values, block_rows, block_cols, test_matrix):
    values = block_values[0, 0]
    side, rank = test_matrix.shape
    half = rank // 2
    n_rows, n_feat = lax.axis_size("rows"), lax.axis_size("feat")
    scale = float(side * n_rows) ** 0.5
    share = side // n_feat
    core = (lax.axis_index("feat") % 2).astype(jnp.int32).reshape(1)

    tile, part = pl.pallas_call(
        sketch_kernel,
        in_specs=[SMEM, SMEM, VMEM, VMEM],
        out_specs=[VMEM, VMEM],
        compiler_params=PARAMS,
        out_shape=[jax.ShapeDtypeStruct((side, side), jnp.bfloat16), f32(n_feat, share, rank)],
    )(block_rows[0, 0], block_cols[0, 0], values, test_matrix)
    sketch = lax.all_gather(jnp.sum(to_each(part, "feat"), axis=0), "feat", axis=0, tiled=True)

    both = pl.pallas_call(
        cosketch_kernel,
        in_specs=[SMEM, VMEM, VMEM],
        out_specs=VMEM,
        compiler_params=PARAMS,
        out_shape=f32(n_rows, 2 * side // n_rows + rank // n_rows, half),
    )(core, tile, sketch)
    both = from_each(jnp.sum(to_each(both, "rows"), axis=0), "rows")

    part, own = pl.pallas_call(
        resketch_kernel,
        in_specs=[VMEM, VMEM],
        out_specs=[VMEM, VMEM],
        compiler_params=PARAMS,
        out_shape=[f32(n_feat, share, rank), f32(rank, half)],
    )(tile, both)
    parts = to_each(part, "feat")
    other = lax.ppermute(own, "feat", [(i, i ^ 1) for i in range(n_feat)])
    inverse = pl.pallas_call(
        factor_kernel,
        in_specs=[SMEM, VMEM, VMEM],
        out_specs=VMEM,
        compiler_params=PARAMS,
        out_shape=f32(rank, rank),
        cost_estimate=pl.CostEstimate(flops=10**10, bytes_accessed=10**6, transcendentals=0),
    )(core, own, other)

    resketch, gram = pl.pallas_call(
        gram_kernel,
        in_specs=[VMEM, VMEM],
        out_specs=[VMEM, VMEM],
        compiler_params=PARAMS,
        out_shape=[f32(share, rank), f32(n_rows, rank // n_rows, rank)],
    )(parts, inverse)
    gram = jnp.sum(to_each(gram, "rows"), axis=0)
    gram = jnp.sum(from_each(gram, "feat"), axis=0)
    return pl.pallas_call(
        lambda *refs: final_kernel(scale, *refs),
        in_specs=[VMEM, VMEM],
        out_specs=VMEM,
        compiler_params=PARAMS,
        out_shape=f32(share, rank),
    )(resketch, from_each(gram, "rows"))


def solution(mesh):
    placed = (
        P("rows", "feat", None, None, None),
        P("rows", "feat", None),
        P("rows", "feat", None),
        P("feat", None),
    )
    return jax.shard_map(
        per_device, mesh=mesh, in_specs=placed, out_specs=P(("rows", "feat"), None), check_vma=False
    )
```

```python
import jax
import jax.numpy as jnp
from jax import lax
from jax.experimental import pallas as pl
from jax.experimental.pallas import tpu as pltpu
from jax.sharding import Mesh, PartitionSpec as P

HIGHEST = lax.Precision.HIGHEST
PARAMS = pltpu.CompilerParams(vmem_limit_bytes=12 * 2**20)
LARGE = pltpu.CompilerParams(vmem_limit_bytes=56 * 2**20)
VMEM = pl.BlockSpec(memory_space=pltpu.VMEM)
SMEM = pl.BlockSpec(memory_space=pltpu.SMEM)
SUB = 8


def dot(a, b, precision=None, contract=(1, 0)):
    dims = (((contract[0],), (contract[1],)), ((), ()))
    return lax.dot_general(a, b, dims, preferred_element_type=jnp.float32, precision=precision)


def terms(x):
    high = x.astype(jnp.bfloat16)
    rest = x - high.astype(jnp.float32)
    mid = rest.astype(jnp.bfloat16)
    return high, mid, (rest - mid.astype(jnp.float32)).astype(jnp.bfloat16)


def dot_terms(tile, x, contract=(1, 0)):
    high, mid, low = terms(x)
    small = dot(tile, mid, contract=contract) + dot(tile, low, contract=contract)
    return dot(tile, high, contract=contract) + small


def block_inverse(block):
    n = block.shape[0]
    shape = (SUB, n)
    parts = [block[i : i + SUB] for i in range(0, n, SUB)]
    lane = lax.broadcasted_iota(jnp.int32, shape, 1)
    sub = lax.broadcasted_iota(jnp.int32, shape, 0)
    full = lambda v: jnp.broadcast_to(v, shape)
    done = []
    for j in range(n // SUB):
        rows = parts[j]
        base = j * SUB
        cols = [full(rows[:, base + k : base + k + 1]) for k in range(SUB)]
        final = jnp.zeros(shape, jnp.float32)
        for k in range(0, SUB, 2):
            a = full(cols[k][k : k + 1, :])
            b = full(cols[k + 1][k : k + 1, :])
            d = full(cols[k + 1][k + 1 : k + 2, :])
            det = a * d - b * b
            inv = 1.0 / det
            first, second = sub == k, sub == k + 1
            own = first | second
            m1 = jnp.where(first, -1.0, jnp.where(second, 0.0, cols[k]))
            m2 = jnp.where(second, -1.0, jnp.where(first, 0.0, cols[k + 1]))
            w1 = m1 * d - m2 * b
            w2 = m2 * a - m1 * b
            for q in range(k + 2, SUB):
                z = w1 * full(cols[q][k : k + 1, :]) + w2 * full(cols[q][k + 1 : k + 2, :])
                cols[q] = jnp.where(own, 0.0, cols[q]) - z * inv
            here, after = lane == base + k, lane == base + k + 1
            r1 = jnp.where(here, 1.0, jnp.where(after, 0.0, full(rows[k : k + 1, :])))
            r2 = jnp.where(after, 1.0, jnp.where(here, 0.0, full(rows[k + 1 : k + 2, :])))
            root = lax.rsqrt(a)
            inv_a = root * root
            u1 = jnp.where(lane <= base + k, r1 * root, 0.0)
            u2 = (r2 - (b * inv_a) * r1) * lax.rsqrt(det * inv_a)
            u2 = jnp.where(lane <= base + k + 1, u2, 0.0)
            final = jnp.where(first, u1, jnp.where(second, u2, final))
            rows = jnp.where(own | here | after, 0.0, rows) - (w1 * r1 + w2 * r2) * inv
        done.append(final)
        pivots = [full(rows[k : k + 1, :]) for k in range(SUB)]
        inside = (lane >= base) & (lane < base + SUB)
        for i in range(j + 1, n // SUB):
            t = [full(parts[i][:, base + k : base + k + 1]) * pivots[k] for k in range(SUB)]
            t = ((t[0] + t[1]) + (t[2] + t[3])) + ((t[4] + t[5]) + (t[6] + t[7]))
            parts[i] = jnp.where(inside, 0.0, parts[i]) - t
    return jnp.concatenate(done, axis=0)


def inverse_factor(gram):
    n = gram.shape[0]
    half = n // 2
    r = lax.broadcasted_iota(jnp.int32, (n, n), 0)
    c = lax.broadcasted_iota(jnp.int32, (n, n), 1)
    diag = jnp.where(r == c, gram, 0.0)
    across = lax.rsqrt(jnp.sum(diag, axis=0, keepdims=True))
    down = lax.rsqrt(jnp.sum(diag, axis=1, keepdims=True))
    unit = jnp.where(r == c, 1.0, gram * across * down)
    first = block_inverse(unit[:half, :half])
    lower = dot(unit[half:, :half], first, HIGHEST, (1, 1))
    second = block_inverse(unit[half:, half:] - dot(lower, lower, HIGHEST, (1, 1)))
    corner = -dot(second, dot(lower, first, HIGHEST), HIGHEST)
    top = jnp.concatenate([first, jnp.zeros_like(first)], axis=1)
    return jnp.concatenate([top, jnp.concatenate([corner, second], axis=1)], axis=0) * across


def pick(core_ref, first, second):
    return jnp.where(core_ref[0] == 0, first, second)


def split_cores(core_ref, product, chips):
    share = product.shape[0] // (2 * chips)
    product = product.reshape(chips, 2, share, product.shape[1])
    even, odd = product[:, 0], product[:, 1]
    return pick(core_ref, even, odd), pick(core_ref, odd, even)


def sketch_kernel(rows_ref, cols_ref, core_ref, values_ref, test_ref, tile_ref, keep_ref, send_ref):
    count, width = values_ref.shape[0], values_ref.shape[1]
    tile_ref[...] = jnp.zeros_like(tile_ref)
    for n in range(count):
        row = pl.multiple_of(rows_ref[n] * width, width)
        col = pl.multiple_of(cols_ref[n] * width, width)
        tile_ref[pl.ds(row, width), pl.ds(col, width)] = values_ref[n]
    product = dot(tile_ref[...], test_ref[...])
    keep_ref[...], send_ref[...] = split_cores(core_ref, product, keep_ref.shape[0])


def cosketch_kernel(core_ref, tile_ref, sketch_ref, out_ref):
    sketch = sketch_ref[...]
    groups, _, half = out_ref.shape
    co = dot_terms(tile_ref[...], sketch, (0, 0))
    split = co.shape[0] // groups
    out_ref[:, :split, :] = co[:, :half].reshape(groups, split, half)
    out_ref[:, split : 2 * split, :] = co[:, half:].reshape(groups, split, half)
    chosen = pick(core_ref, sketch[:, :half], sketch[:, half:])
    gram = dot(sketch, chosen, HIGHEST, (0, 0))
    out_ref[:, 2 * split :, :] = gram.reshape(groups, gram.shape[0] // groups, half)


def resketch_kernel(core_ref, tile_ref, both_ref, keep_ref, send_ref, gram_ref):
    both = both_ref[...]
    side = tile_ref.shape[0]
    chips, share, rank = keep_ref.shape
    half = rank // 2
    split = side // both.shape[0]
    left = both[:, :split, :].reshape(side, half)
    right = both[:, split : 2 * split, :].reshape(side, half)
    product = dot_terms(tile_ref[...], jnp.concatenate([left, right], axis=1))
    keep_ref[...], send_ref[:, :share, :] = split_cores(core_ref, product, chips)
    gram = both[:, 2 * split :, :].reshape(rank, half)
    gram_ref[...] = gram
    wide = jnp.concatenate([gram[:half], gram[half:]], axis=1)
    send_ref[:, share:, :] = wide.reshape(chips, half // chips, rank)


def factor_kernel(core_ref, own_ref, received_ref, out_ref):
    rank, half = own_ref.shape
    share = received_ref.shape[1] - half // received_ref.shape[0]
    wide = received_ref[:, share:, :].reshape(half, rank)
    own, other = own_ref[...], jnp.concatenate([wide[:, :half], wide[:, half:]], axis=0)
    gram = jnp.concatenate([pick(core_ref, own, other), pick(core_ref, other, own)], axis=1)
    out_ref[...] = inverse_factor(gram)


def gram_kernel(parts_ref, inverse_ref, share_ref, gram_ref):
    share = dot(jnp.sum(parts_ref[...], axis=0), inverse_ref[...], HIGHEST, (1, 1))
    share_ref[...] = share
    gram_ref[...] = dot(share, share, HIGHEST, (0, 0)).reshape(gram_ref.shape)


def final_kernel(scale, share_ref, gram_ref, out_ref):
    rank = out_ref.shape[1]
    inverse = inverse_factor(gram_ref[...].reshape(rank, rank))
    out_ref[...] = dot(share_ref[...], inverse, HIGHEST, (1, 1)) * scale


FEAT = ("y", "core")


def to_each(x, axis):
    return lax.all_to_all(x, axis, 0, 0, tiled=True)


def from_each(x, axis):
    size = lax.axis_size(axis)
    return to_each(jnp.broadcast_to(x[None], (size,) + x.shape), axis)


def swap_cores(x):
    return lax.ppermute(x, "core", [(0, 1), (1, 0)])


def f32(*shape):
    return jax.ShapeDtypeStruct(shape, jnp.float32)


def per_device(block_values, block_rows, block_cols, test_matrix):
    values = block_values[0, 0]
    side, rank = test_matrix.shape
    half = rank // 2
    n_rows, chips = lax.axis_size("rows"), lax.axis_size("y")
    scale = float(side * n_rows) ** 0.5
    share = side // (2 * chips)
    core = lax.axis_index("core").astype(jnp.int32).reshape(1)

    tile, keep, send = pl.pallas_call(
        sketch_kernel,
        in_specs=[SMEM, SMEM, SMEM, VMEM, VMEM],
        out_specs=[VMEM] * 3,
        out_shape=[jax.ShapeDtypeStruct((side, side), jnp.bfloat16)] + [f32(chips, share, rank)] * 2,
        compiler_params=LARGE,
    )(block_rows[0, 0], block_cols[0, 0], core, values, test_matrix)
    sketch = jnp.sum(to_each(keep + swap_cores(send), "y"), axis=0)
    sketch = lax.all_gather(sketch, FEAT, axis=0, tiled=True)

    both = pl.pallas_call(
        cosketch_kernel,
        in_specs=[SMEM, VMEM, VMEM],
        out_specs=VMEM,
        out_shape=f32(n_rows, 2 * side // n_rows + rank // n_rows, half),
        compiler_params=PARAMS,
    )(core, tile, sketch)
    both = from_each(jnp.sum(to_each(both, "rows"), axis=0), "rows")

    keep, send, own = pl.pallas_call(
        resketch_kernel,
        in_specs=[SMEM, VMEM, VMEM],
        out_specs=[VMEM] * 3,
        out_shape=[f32(chips, share, rank), f32(chips, share + half // chips, rank), f32(rank, half)],
        compiler_params=PARAMS,
    )(core, tile, both)
    received = swap_cores(send)
    parts = to_each(keep + received[:, :share], "y")
    inverse = pl.pallas_call(
        factor_kernel,
        in_specs=[SMEM, VMEM, VMEM],
        out_specs=VMEM,
        out_shape=f32(rank, rank),
        compiler_params=PARAMS,
        cost_estimate=pl.CostEstimate(flops=10**10, bytes_accessed=10**6, transcendentals=0),
    )(core, own, received)

    resketch, gram = pl.pallas_call(
        gram_kernel,
        in_specs=[VMEM] * 2,
        out_specs=[VMEM] * 2,
        out_shape=[f32(share, rank), f32(n_rows, rank // n_rows, rank)],
        compiler_params=PARAMS,
    )(parts, inverse)
    gram = jnp.sum(to_each(gram, "rows"), axis=0)
    gram = jnp.sum(from_each(gram, FEAT), axis=0)
    return pl.pallas_call(
        lambda *refs: final_kernel(scale, *refs),
        in_specs=[VMEM] * 2,
        out_specs=VMEM,
        out_shape=f32(share, rank),
        compiler_params=PARAMS,
    )(resketch, from_each(gram, "rows"))


def solution(mesh):
    n_rows, n_feat = mesh.devices.shape
    chips = Mesh(mesh.devices.reshape(n_rows, n_feat // 2, 2), ("rows",) + FEAT)
    placed = (
        P("rows", FEAT, None, None, None),
        P("rows", FEAT, None),
        P("rows", FEAT, None),
        P(FEAT, None),
    )
    return jax.shard_map(
        per_device, mesh=chips, in_specs=placed, out_specs=P(("rows",) + FEAT, None), check_vma=False
    )
```

```python
import jax
import jax.numpy as jnp
from jax import lax
from jax.experimental import pallas as pl
from jax.experimental.pallas import tpu as pltpu
from jax.sharding import Mesh, PartitionSpec as P

HIGHEST = lax.Precision.HIGHEST
PARAMS = pltpu.CompilerParams(vmem_limit_bytes=12 * 2**20)
LARGE = pltpu.CompilerParams(vmem_limit_bytes=56 * 2**20)
VMEM = pl.BlockSpec(memory_space=pltpu.VMEM)
SMEM = pl.BlockSpec(memory_space=pltpu.SMEM)
SUB = 16


def dot(a, b, precision=None, contract=(1, 0)):
    dims = (((contract[0],), (contract[1],)), ((), ()))
    return lax.dot_general(a, b, dims, preferred_element_type=jnp.float32, precision=precision)


def terms(x):
    high = x.astype(jnp.bfloat16)
    rest = x - high.astype(jnp.float32)
    mid = rest.astype(jnp.bfloat16)
    return high, mid, (rest - mid.astype(jnp.float32)).astype(jnp.bfloat16)


def dot_terms(tile, x, contract=(1, 0)):
    high, mid, low = terms(x)
    small = dot(tile, mid, contract=contract) + dot(tile, low, contract=contract)
    return dot(tile, high, contract=contract) + small


def block_inverse(block):
    n = block.shape[0]
    shape = (SUB, n)
    parts = [block[i : i + SUB] for i in range(0, n, SUB)]
    lane = lax.broadcasted_iota(jnp.int32, shape, 1)
    sub = lax.broadcasted_iota(jnp.int32, shape, 0)
    full = lambda v: jnp.broadcast_to(v, shape)
    done = []
    for j in range(n // SUB):
        rows = parts[j]
        base = j * SUB
        cols = [full(rows[:, base + k : base + k + 1]) for k in range(SUB)]
        final = jnp.zeros(shape, jnp.float32)
        for k in range(0, SUB, 2):
            a = full(cols[k][k : k + 1, :])
            b = full(cols[k + 1][k : k + 1, :])
            d = full(cols[k + 1][k + 1 : k + 2, :])
            det = a * d - b * b
            inv = 1.0 / det
            first, second = sub == k, sub == k + 1
            own = first | second
            m1 = jnp.where(first, -1.0, jnp.where(second, 0.0, cols[k]))
            m2 = jnp.where(second, -1.0, jnp.where(first, 0.0, cols[k + 1]))
            w1 = m1 * d - m2 * b
            w2 = m2 * a - m1 * b
            for q in range(k + 2, SUB):
                z = w1 * full(cols[q][k : k + 1, :]) + w2 * full(cols[q][k + 1 : k + 2, :])
                cols[q] = jnp.where(own, 0.0, cols[q]) - z * inv
            here, after = lane == base + k, lane == base + k + 1
            r1 = jnp.where(here, 1.0, jnp.where(after, 0.0, full(rows[k : k + 1, :])))
            r2 = jnp.where(after, 1.0, jnp.where(here, 0.0, full(rows[k + 1 : k + 2, :])))
            root = lax.rsqrt(a)
            inv_a = root * root
            u1 = jnp.where(lane <= base + k, r1 * root, 0.0)
            u2 = (r2 - (b * inv_a) * r1) * lax.rsqrt(det * inv_a)
            u2 = jnp.where(lane <= base + k + 1, u2, 0.0)
            final = jnp.where(first, u1, jnp.where(second, u2, final))
            rows = jnp.where(own | here | after, 0.0, rows) - (w1 * r1 + w2 * r2) * inv
        done.append(final)
        pivots = [full(rows[k : k + 1, :]) for k in range(SUB)]
        if j + 1 < n // SUB:
            t = [full(parts[j + 1][:, base + k : base + k + 1]) * pivots[k] for k in range(SUB)]
            while len(t) > 1:
                t = [t[i] + t[i + 1] for i in range(0, len(t), 2)]
            inside = (lane >= base) & (lane < base + SUB)
            parts[j + 1] = jnp.where(inside, 0.0, parts[j + 1]) - t[0]
        if j + 2 < n // SUB:
            rest = jnp.concatenate(parts[j + 2 :], axis=0)
            spread = [jnp.zeros((base, n), jnp.float32)] if base else []
            spread += [rows, jnp.zeros((n - base - SUB, n), jnp.float32)]
            wide = lax.broadcasted_iota(jnp.int32, rest.shape, 1)
            inside = (wide >= base) & (wide < base + SUB)
            change = dot(jnp.where(inside, rest, 0.0), jnp.concatenate(spread, axis=0), HIGHEST)
            rest = jnp.where(inside, 0.0, rest) - change
            parts[j + 2 :] = [rest[i : i + SUB] for i in range(0, rest.shape[0], SUB)]
    return jnp.concatenate(done, axis=0)


def factor(gram):
    n = gram.shape[0]
    half = n // 2
    r = lax.broadcasted_iota(jnp.int32, (n, n), 0)
    c = lax.broadcasted_iota(jnp.int32, (n, n), 1)
    diag = jnp.where(r == c, gram, 0.0)
    across = lax.rsqrt(jnp.sum(diag, axis=0, keepdims=True))
    down = lax.rsqrt(jnp.sum(diag, axis=1, keepdims=True))
    unit = jnp.where(r == c, 1.0, gram * across * down)
    first = block_inverse(unit[:half, :half])
    lower = dot(unit[half:, :half], first, HIGHEST, (1, 1))
    second = block_inverse(unit[half:, half:] - dot(lower, lower, HIGHEST, (1, 1)))
    return across, first, lower, second


def inverse_factor(gram):
    across, first, lower, second = factor(gram)
    corner = -dot(second, dot(lower, first, HIGHEST), HIGHEST)
    top = jnp.concatenate([first, jnp.zeros_like(first)], axis=1)
    return jnp.concatenate([top, jnp.concatenate([corner, second], axis=1)], axis=0) * across


def whiten(x, gram):
    across, first, lower, second = factor(gram)
    half = first.shape[0]
    x = x * across
    left = dot(x[:, :half], first, HIGHEST, (1, 1))
    right = dot(x[:, half:] - dot(left, lower, HIGHEST, (1, 1)), second, HIGHEST, (1, 1))
    return jnp.concatenate([left, right], axis=1)


def pick(core_ref, first, second):
    return jnp.where(core_ref[0] == 0, first, second)


def split_cores(core_ref, product, chips):
    share = product.shape[0] // (2 * chips)
    product = product.reshape(chips, 2, share, product.shape[1])
    even, odd = product[:, 0], product[:, 1]
    return pick(core_ref, even, odd), pick(core_ref, odd, even)


def sketch_kernel(rows_ref, cols_ref, core_ref, values_ref, test_ref, tile_ref, keep_ref, send_ref):
    count, width = values_ref.shape[0], values_ref.shape[1]
    tile_ref[...] = jnp.zeros_like(tile_ref)
    for n in range(count):
        row = pl.multiple_of(rows_ref[n] * width, width)
        col = pl.multiple_of(cols_ref[n] * width, width)
        tile_ref[pl.ds(row, width), pl.ds(col, width)] = values_ref[n]
    product = dot(tile_ref[...], test_ref[...])
    keep_ref[...], send_ref[...] = split_cores(core_ref, product, keep_ref.shape[0])


def cosketch_kernel(core_ref, tile_ref, sketch_ref, out_ref):
    sketch = sketch_ref[...]
    groups, _, half = out_ref.shape
    co = dot_terms(tile_ref[...], sketch, (0, 0))
    split = co.shape[0] // groups
    out_ref[:, :split, :] = co[:, :half].reshape(groups, split, half)
    out_ref[:, split : 2 * split, :] = co[:, half:].reshape(groups, split, half)
    chosen = pick(core_ref, sketch[:, :half], sketch[:, half:])
    gram = dot(sketch, chosen, HIGHEST, (0, 0))
    out_ref[:, 2 * split :, :] = gram.reshape(groups, gram.shape[0] // groups, half)


def resketch_kernel(core_ref, tile_ref, both_ref, keep_ref, send_ref, gram_ref):
    both = both_ref[...]
    side = tile_ref.shape[0]
    chips, share, rank = keep_ref.shape
    half = rank // 2
    split = side // both.shape[0]
    left = both[:, :split, :].reshape(side, half)
    right = both[:, split : 2 * split, :].reshape(side, half)
    product = dot_terms(tile_ref[...], jnp.concatenate([left, right], axis=1))
    keep_ref[...], send_ref[:, :share, :] = split_cores(core_ref, product, chips)
    gram = both[:, 2 * split :, :].reshape(rank, half)
    gram_ref[...] = gram
    wide = jnp.concatenate([gram[:half], gram[half:]], axis=1)
    send_ref[:, share:, :] = wide.reshape(chips, half // chips, rank)


def factor_kernel(core_ref, own_ref, received_ref, out_ref):
    rank, half = own_ref.shape
    share = received_ref.shape[1] - half // received_ref.shape[0]
    wide = received_ref[:, share:, :].reshape(half, rank)
    own, other = own_ref[...], jnp.concatenate([wide[:, :half], wide[:, half:]], axis=0)
    gram = jnp.concatenate([pick(core_ref, own, other), pick(core_ref, other, own)], axis=1)
    out_ref[...] = inverse_factor(gram)


def gram_kernel(parts_ref, inverse_ref, share_ref, gram_ref):
    share = dot(jnp.sum(parts_ref[...], axis=0), inverse_ref[...], HIGHEST, (1, 1))
    share_ref[...] = share
    gram_ref[...] = dot(share, share, HIGHEST, (0, 0)).reshape(gram_ref.shape)


def final_kernel(scale, share_ref, gram_ref, out_ref):
    rank = out_ref.shape[1]
    out_ref[...] = whiten(share_ref[...], gram_ref[...].reshape(rank, rank)) * scale


FEAT = ("y", "core")


def to_each(x, axis):
    return lax.all_to_all(x, axis, 0, 0, tiled=True)


def from_each(x, axis):
    size = lax.axis_size(axis)
    return to_each(jnp.broadcast_to(x[None], (size,) + x.shape), axis)


def swap_cores(x):
    return lax.ppermute(x, "core", [(0, 1), (1, 0)])


def f32(*shape):
    return jax.ShapeDtypeStruct(shape, jnp.float32)


def per_device(block_values, block_rows, block_cols, test_matrix):
    values = block_values[0, 0]
    side, rank = test_matrix.shape
    half = rank // 2
    n_rows, chips = lax.axis_size("rows"), lax.axis_size("y")
    scale = float(side * n_rows) ** 0.5
    share = side // (2 * chips)
    core = lax.axis_index("core").astype(jnp.int32).reshape(1)

    tile, keep, send = pl.pallas_call(
        sketch_kernel,
        in_specs=[SMEM, SMEM, SMEM, VMEM, VMEM],
        out_specs=[VMEM] * 3,
        out_shape=[jax.ShapeDtypeStruct((side, side), jnp.bfloat16)] + [f32(chips, share, rank)] * 2,
        compiler_params=LARGE,
    )(block_rows[0, 0], block_cols[0, 0], core, values, test_matrix)
    sketch = jnp.sum(to_each(keep + swap_cores(send), "y"), axis=0)
    sketch = lax.all_gather(sketch, FEAT, axis=0, tiled=True)

    both = pl.pallas_call(
        cosketch_kernel,
        in_specs=[SMEM, VMEM, VMEM],
        out_specs=VMEM,
        out_shape=f32(n_rows, 2 * side // n_rows + rank // n_rows, half),
        compiler_params=PARAMS,
    )(core, tile, sketch)
    both = from_each(jnp.sum(to_each(both, "rows"), axis=0), "rows")

    keep, send, own = pl.pallas_call(
        resketch_kernel,
        in_specs=[SMEM, VMEM, VMEM],
        out_specs=[VMEM] * 3,
        out_shape=[f32(chips, share, rank), f32(chips, share + half // chips, rank), f32(rank, half)],
        compiler_params=PARAMS,
    )(core, tile, both)
    received = swap_cores(send)
    parts = to_each(keep + received[:, :share], "y")
    inverse = pl.pallas_call(
        factor_kernel,
        in_specs=[SMEM, VMEM, VMEM],
        out_specs=VMEM,
        out_shape=f32(rank, rank),
        compiler_params=PARAMS,
        cost_estimate=pl.CostEstimate(flops=10**10, bytes_accessed=10**6, transcendentals=0),
    )(core, own, received)

    resketch, gram = pl.pallas_call(
        gram_kernel,
        in_specs=[VMEM] * 2,
        out_specs=[VMEM] * 2,
        out_shape=[f32(share, rank), f32(n_rows, rank // n_rows, rank)],
        compiler_params=PARAMS,
    )(parts, inverse)
    gram = jnp.sum(to_each(gram, "rows"), axis=0)
    gram = jnp.sum(from_each(gram, FEAT), axis=0)
    return pl.pallas_call(
        lambda *refs: final_kernel(scale, *refs),
        in_specs=[VMEM] * 2,
        out_specs=VMEM,
        out_shape=f32(share, rank),
        compiler_params=PARAMS,
    )(resketch, from_each(gram, "rows"))


def solution(mesh):
    n_rows, n_feat = mesh.devices.shape
    chips = Mesh(mesh.devices.reshape(n_rows, n_feat // 2, 2), ("rows",) + FEAT)
    placed = (
        P("rows", FEAT, None, None, None),
        P("rows", FEAT, None),
        P("rows", FEAT, None),
        P(FEAT, None),
    )
    return jax.shard_map(
        per_device, mesh=chips, in_specs=placed, out_specs=P(("rows",) + FEAT, None), check_vma=False
    )
```

```python
import jax
import jax.numpy as jnp
from jax import lax
from jax.experimental import pallas as pl
from jax.experimental.pallas import tpu as pltpu
from jax.sharding import Mesh, PartitionSpec as P

HIGHEST = lax.Precision.HIGHEST
PARAMS = pltpu.CompilerParams(vmem_limit_bytes=12 * 2**20)
LARGE = pltpu.CompilerParams(vmem_limit_bytes=56 * 2**20)
VMEM = pl.BlockSpec(memory_space=pltpu.VMEM)
SMEM = pl.BlockSpec(memory_space=pltpu.SMEM)
SUB = 16


def dot(a, b, precision=None, contract=(1, 0)):
    dims = (((contract[0],), (contract[1],)), ((), ()))
    return lax.dot_general(a, b, dims, preferred_element_type=jnp.float32, precision=precision)


def terms(x):
    high = x.astype(jnp.bfloat16)
    rest = x - high.astype(jnp.float32)
    mid = rest.astype(jnp.bfloat16)
    return high, mid, (rest - mid.astype(jnp.float32)).astype(jnp.bfloat16)


def dot_terms(tile, x, contract=(1, 0)):
    high, mid, low = terms(x)
    small = dot(tile, mid, contract=contract) + dot(tile, low, contract=contract)
    return dot(tile, high, contract=contract) + small


def block_inverse(block):
    n = block.shape[0]
    shape = (SUB, n)
    parts = [block[i : i + SUB] for i in range(0, n, SUB)]
    lane = lax.broadcasted_iota(jnp.int32, shape, 1)
    sub = lax.broadcasted_iota(jnp.int32, shape, 0)
    full = lambda v: jnp.broadcast_to(v, shape)
    done = []
    for j in range(n // SUB):
        rows = parts[j]
        base = j * SUB
        cols = [full(rows[:, base + k : base + k + 1]) for k in range(SUB)]
        final = jnp.zeros(shape, jnp.float32)
        for k in range(0, SUB, 2):
            a = full(cols[k][k : k + 1, :])
            b = full(cols[k + 1][k : k + 1, :])
            d = full(cols[k + 1][k + 1 : k + 2, :])
            det = a * d - b * b
            inv = 1.0 / det
            first, second = sub == k, sub == k + 1
            own = first | second
            m1 = jnp.where(first, -1.0, jnp.where(second, 0.0, cols[k]))
            m2 = jnp.where(second, -1.0, jnp.where(first, 0.0, cols[k + 1]))
            w1 = m1 * d - m2 * b
            w2 = m2 * a - m1 * b
            for q in range(k + 2, SUB):
                z = w1 * full(cols[q][k : k + 1, :]) + w2 * full(cols[q][k + 1 : k + 2, :])
                cols[q] = jnp.where(own, 0.0, cols[q]) - z * inv
            here, after = lane == base + k, lane == base + k + 1
            r1 = jnp.where(here, 1.0, jnp.where(after, 0.0, full(rows[k : k + 1, :])))
            r2 = jnp.where(after, 1.0, jnp.where(here, 0.0, full(rows[k + 1 : k + 2, :])))
            root = lax.rsqrt(a)
            inv_a = root * root
            u1 = jnp.where(lane <= base + k, r1 * root, 0.0)
            u2 = (r2 - (b * inv_a) * r1) * lax.rsqrt(det * inv_a)
            u2 = jnp.where(lane <= base + k + 1, u2, 0.0)
            final = jnp.where(first, u1, jnp.where(second, u2, final))
            rows = jnp.where(own | here | after, 0.0, rows) - (w1 * r1 + w2 * r2) * inv
        done.append(final)
        pivots = [full(rows[k : k + 1, :]) for k in range(SUB)]
        if j + 1 < n // SUB:
            t = [full(parts[j + 1][:, base + k : base + k + 1]) * pivots[k] for k in range(SUB)]
            while len(t) > 1:
                t = [t[i] + t[i + 1] for i in range(0, len(t), 2)]
            inside = (lane >= base) & (lane < base + SUB)
            parts[j + 1] = jnp.where(inside, 0.0, parts[j + 1]) - t[0]
        if j + 2 < n // SUB:
            rest = jnp.concatenate(parts[j + 2 :], axis=0)
            spread = [jnp.zeros((base, n), jnp.float32)] if base else []
            spread += [rows, jnp.zeros((n - base - SUB, n), jnp.float32)]
            wide = lax.broadcasted_iota(jnp.int32, rest.shape, 1)
            inside = (wide >= base) & (wide < base + SUB)
            change = dot(jnp.where(inside, rest, 0.0), jnp.concatenate(spread, axis=0), HIGHEST)
            rest = jnp.where(inside, 0.0, rest) - change
            parts[j + 2 :] = [rest[i : i + SUB] for i in range(0, rest.shape[0], SUB)]
    return jnp.concatenate(done, axis=0)


def factor(first, lower, second):
    n = first.shape[0]
    r = lax.broadcasted_iota(jnp.int32, (n, n), 0)
    c = lax.broadcasted_iota(jnp.int32, (n, n), 1)
    scales = []
    for block in (first, second):
        diag = jnp.where(r == c, block, 0.0)
        scales.append([lax.rsqrt(jnp.sum(diag, axis=i, keepdims=True)) for i in (0, 1)])
    (across1, down1), (across2, down2) = scales
    inv1 = block_inverse(jnp.where(r == c, 1.0, first * across1 * down1))
    lower = dot(lower * across1 * down2, inv1, HIGHEST, (1, 1))
    second = jnp.where(r == c, 1.0, second * across2 * down2)
    inv2 = block_inverse(second - dot(lower, lower, HIGHEST, (1, 1)))
    return across1, across2, inv1, lower, inv2


def inverse_factor(gram):
    half = gram.shape[0] // 2
    across1, across2, inv1, lower, inv2 = factor(gram[:half, :half], gram[half:, :half], gram[half:, half:])
    corner = -dot(inv2, dot(lower, inv1, HIGHEST), HIGHEST)
    left = jnp.concatenate([inv1, corner], axis=0) * across1
    right = jnp.concatenate([jnp.zeros_like(inv2), inv2], axis=0) * across2
    return jnp.concatenate([left, right], axis=1)


def whiten(x, *blocks):
    across1, across2, inv1, lower, inv2 = factor(*blocks)
    half = inv1.shape[0]
    left = dot(x[:, :half] * across1, inv1, HIGHEST, (1, 1))
    right = x[:, half:] * across2 - dot(left, lower, HIGHEST, (1, 1))
    return jnp.concatenate([left, dot(right, inv2, HIGHEST, (1, 1))], axis=1)


def pick(core_ref, first, second):
    return jnp.where(core_ref[0] == 0, first, second)


def split_cores(core_ref, product, chips):
    share = product.shape[0] // (2 * chips)
    product = product.reshape(chips, 2, share, product.shape[1])
    even, odd = product[:, 0], product[:, 1]
    return pick(core_ref, even, odd), pick(core_ref, odd, even)


def sketch_kernel(rows_ref, cols_ref, core_ref, values_ref, test_ref, tile_ref, keep_ref, send_ref):
    count, width = values_ref.shape[0], values_ref.shape[1]
    tile_ref[...] = jnp.zeros_like(tile_ref)
    for n in range(count):
        row = pl.multiple_of(rows_ref[n] * width, width)
        col = pl.multiple_of(cols_ref[n] * width, width)
        tile_ref[pl.ds(row, width), pl.ds(col, width)] = values_ref[n]
    product = dot(tile_ref[...], test_ref[...])
    keep_ref[...], send_ref[...] = split_cores(core_ref, product, keep_ref.shape[0])


def cosketch_kernel(core_ref, tile_ref, sketch_ref, out_ref):
    sketch = sketch_ref[...]
    groups, _, half = out_ref.shape
    co = dot_terms(tile_ref[...], sketch, (0, 0))
    split = co.shape[0] // groups
    out_ref[:, :split, :] = co[:, :half].reshape(groups, split, half)
    out_ref[:, split : 2 * split, :] = co[:, half:].reshape(groups, split, half)
    chosen = pick(core_ref, sketch[:, :half], sketch[:, half:])
    gram = dot(sketch, chosen, HIGHEST, (0, 0))
    out_ref[:, 2 * split :, :] = gram.reshape(groups, gram.shape[0] // groups, half)


def resketch_kernel(core_ref, tile_ref, both_ref, keep_ref, send_ref, gram_ref):
    both = both_ref[...]
    side = tile_ref.shape[0]
    chips, share, rank = keep_ref.shape
    half = rank // 2
    split = side // both.shape[0]
    left = both[:, :split, :].reshape(side, half)
    right = both[:, split : 2 * split, :].reshape(side, half)
    product = dot_terms(tile_ref[...], jnp.concatenate([left, right], axis=1))
    keep_ref[...], send_ref[:, :share, :] = split_cores(core_ref, product, chips)
    gram = both[:, 2 * split :, :].reshape(rank, half)
    gram_ref[...] = gram
    wide = jnp.concatenate([gram[:half], gram[half:]], axis=1)
    send_ref[:, share:, :] = wide.reshape(chips, half // chips, rank)


def factor_kernel(core_ref, own_ref, received_ref, out_ref):
    rank, half = own_ref.shape
    share = received_ref.shape[1] - half // received_ref.shape[0]
    wide = received_ref[:, share:, :].reshape(half, rank)
    own, other = own_ref[...], jnp.concatenate([wide[:, :half], wide[:, half:]], axis=0)
    gram = jnp.concatenate([pick(core_ref, own, other), pick(core_ref, other, own)], axis=1)
    out_ref[...] = inverse_factor(gram)


def gram_kernel(parts_ref, inverse_ref, share_ref, gram_ref):
    share = dot(jnp.sum(parts_ref[...], axis=0), inverse_ref[...], HIGHEST, (1, 1))
    share_ref[...] = share
    gram = dot(share, share, HIGHEST, (0, 0))
    half = gram.shape[0] // 2
    gram_ref[: 2 * half, :] = gram[:, :half]
    gram_ref[2 * half :, :] = gram[half:, half:]


def final_kernel(scale, share_ref, gram_ref, out_ref):
    gram = gram_ref[...]
    half = gram.shape[1]
    first, lower, second = gram[:half], gram[half : 2 * half], gram[2 * half :]
    out_ref[...] = whiten(share_ref[...], first, lower, second) * scale


FEAT = ("y", "core")


def to_each(x, axis):
    return lax.all_to_all(x, axis, 0, 0, tiled=True)


def from_each(x, axis):
    size = lax.axis_size(axis)
    return to_each(jnp.broadcast_to(x[None], (size,) + x.shape), axis)


def swap_cores(x):
    return lax.ppermute(x, "core", [(0, 1), (1, 0)])


def f32(*shape):
    return jax.ShapeDtypeStruct(shape, jnp.float32)


def per_device(block_values, block_rows, block_cols, test_matrix):
    values = block_values[0, 0]
    side, rank = test_matrix.shape
    half = rank // 2
    n_rows, chips = lax.axis_size("rows"), lax.axis_size("y")
    scale = float(side * n_rows) ** 0.5
    share = side // (2 * chips)
    core = lax.axis_index("core").astype(jnp.int32).reshape(1)

    tile, keep, send = pl.pallas_call(
        sketch_kernel,
        in_specs=[SMEM, SMEM, SMEM, VMEM, VMEM],
        out_specs=[VMEM] * 3,
        out_shape=[jax.ShapeDtypeStruct((side, side), jnp.bfloat16)] + [f32(chips, share, rank)] * 2,
        compiler_params=LARGE,
    )(block_rows[0, 0], block_cols[0, 0], core, values, test_matrix)
    sketch = jnp.sum(to_each(keep + swap_cores(send), "y"), axis=0)
    sketch = lax.all_gather(sketch, FEAT, axis=0, tiled=True)

    both = pl.pallas_call(
        cosketch_kernel,
        in_specs=[SMEM, VMEM, VMEM],
        out_specs=VMEM,
        out_shape=f32(n_rows, 2 * side // n_rows + rank // n_rows, half),
        compiler_params=PARAMS,
    )(core, tile, sketch)
    both = from_each(jnp.sum(to_each(both, "rows"), axis=0), "rows")

    keep, send, own = pl.pallas_call(
        resketch_kernel,
        in_specs=[SMEM, VMEM, VMEM],
        out_specs=[VMEM] * 3,
        out_shape=[f32(chips, share, rank), f32(chips, share + half // chips, rank), f32(rank, half)],
        compiler_params=PARAMS,
    )(core, tile, both)
    received = swap_cores(send)
    parts = to_each(keep + received[:, :share], "y")
    inverse = pl.pallas_call(
        factor_kernel,
        in_specs=[SMEM, VMEM, VMEM],
        out_specs=VMEM,
        out_shape=f32(rank, rank),
        compiler_params=PARAMS,
        cost_estimate=pl.CostEstimate(flops=10**10, bytes_accessed=10**6, transcendentals=0),
    )(core, own, received)

    resketch, gram = pl.pallas_call(
        gram_kernel,
        in_specs=[VMEM] * 2,
        out_specs=[VMEM] * 2,
        out_shape=[f32(share, rank), f32(3 * half, half)],
        compiler_params=PARAMS,
    )(parts, inverse)
    gram = gram.reshape(n_rows, 3 * half // (4 * n_rows), 4, half)
    gram = jnp.sum(to_each(gram, "rows"), axis=0)
    gram = jnp.sum(from_each(gram, FEAT), axis=0)
    return pl.pallas_call(
        lambda *refs: final_kernel(scale, *refs),
        in_specs=[VMEM] * 2,
        out_specs=VMEM,
        out_shape=f32(share, rank),
        compiler_params=PARAMS,
    )(resketch, from_each(gram, "rows").reshape(3 * half, half))


def solution(mesh):
    n_rows, n_feat = mesh.devices.shape
    chips = Mesh(mesh.devices.reshape(n_rows, n_feat // 2, 2), ("rows",) + FEAT)
    placed = (
        P("rows", FEAT, None, None, None),
        P("rows", FEAT, None),
        P("rows", FEAT, None),
        P(FEAT, None),
    )
    return jax.shard_map(
        per_device, mesh=chips, in_specs=placed, out_specs=P(("rows",) + FEAT, None), check_vma=False
    )
```

```python
import jax
import jax.numpy as jnp
from jax import lax
from jax.experimental import pallas as pl
from jax.experimental.pallas import tpu as pltpu
from jax.sharding import Mesh, PartitionSpec as P

HIGHEST = lax.Precision.HIGHEST
PARAMS = pltpu.CompilerParams(vmem_limit_bytes=12 * 2**20)
LARGE = pltpu.CompilerParams(vmem_limit_bytes=56 * 2**20)
VMEM = pl.BlockSpec(memory_space=pltpu.VMEM)
SMEM = pl.BlockSpec(memory_space=pltpu.SMEM)
SUB = 16


def dot(a, b, precision=None, contract=(1, 0)):
    dims = (((contract[0],), (contract[1],)), ((), ()))
    return lax.dot_general(a, b, dims, preferred_element_type=jnp.float32, precision=precision)


def terms(x):
    high = x.astype(jnp.bfloat16)
    rest = x - high.astype(jnp.float32)
    mid = rest.astype(jnp.bfloat16)
    return high, mid, (rest - mid.astype(jnp.float32)).astype(jnp.bfloat16)


def dot_terms(tile, x, contract=(1, 0)):
    high, mid, low = terms(x)
    small = dot(tile, mid, contract=contract) + dot(tile, low, contract=contract)
    return dot(tile, high, contract=contract) + small


def block_inverse(block):
    n = block.shape[0]
    shape = (SUB, n)
    parts = [block[i : i + SUB] for i in range(0, n, SUB)]
    lane = lax.broadcasted_iota(jnp.int32, shape, 1)
    sub = lax.broadcasted_iota(jnp.int32, shape, 0)
    full = lambda v: jnp.broadcast_to(v, shape)
    done = []
    for j in range(n // SUB):
        rows = parts[j]
        base = j * SUB
        cols = [full(rows[:, base + k : base + k + 1]) for k in range(SUB)]
        final = jnp.zeros(shape, jnp.float32)
        for k in range(0, SUB, 2):
            a = full(cols[k][k : k + 1, :])
            b = full(cols[k + 1][k : k + 1, :])
            d = full(cols[k + 1][k + 1 : k + 2, :])
            det = a * d - b * b
            inv = 1.0 / det
            first, second = sub == k, sub == k + 1
            own = first | second
            m1 = jnp.where(first, -1.0, jnp.where(second, 0.0, cols[k]))
            m2 = jnp.where(second, -1.0, jnp.where(first, 0.0, cols[k + 1]))
            w1 = m1 * d - m2 * b
            w2 = m2 * a - m1 * b
            for q in range(k + 2, SUB):
                z = w1 * full(cols[q][k : k + 1, :]) + w2 * full(cols[q][k + 1 : k + 2, :])
                cols[q] = jnp.where(own, 0.0, cols[q]) - z * inv
            here, after = lane == base + k, lane == base + k + 1
            r1 = jnp.where(here, 1.0, jnp.where(after, 0.0, full(rows[k : k + 1, :])))
            r2 = jnp.where(after, 1.0, jnp.where(here, 0.0, full(rows[k + 1 : k + 2, :])))
            root = lax.rsqrt(a)
            inv_a = root * root
            u1 = jnp.where(lane <= base + k, r1 * root, 0.0)
            u2 = (r2 - (b * inv_a) * r1) * lax.rsqrt(det * inv_a)
            u2 = jnp.where(lane <= base + k + 1, u2, 0.0)
            final = jnp.where(first, u1, jnp.where(second, u2, final))
            rows = jnp.where(own | here | after, 0.0, rows) - (w1 * r1 + w2 * r2) * inv
        done.append(final)
        pivots = [full(rows[k : k + 1, :]) for k in range(SUB)]
        if j + 1 < n // SUB:
            t = [full(parts[j + 1][:, base + k : base + k + 1]) * pivots[k] for k in range(SUB)]
            while len(t) > 1:
                t = [t[i] + t[i + 1] for i in range(0, len(t), 2)]
            inside = (lane >= base) & (lane < base + SUB)
            parts[j + 1] = jnp.where(inside, 0.0, parts[j + 1]) - t[0]
        if j + 2 < n // SUB:
            rest = jnp.concatenate(parts[j + 2 :], axis=0)
            spread = [jnp.zeros((base, n), jnp.float32)] if base else []
            spread += [rows, jnp.zeros((n - base - SUB, n), jnp.float32)]
            wide = lax.broadcasted_iota(jnp.int32, rest.shape, 1)
            inside = (wide >= base) & (wide < base + SUB)
            change = dot(jnp.where(inside, rest, 0.0), jnp.concatenate(spread, axis=0), HIGHEST)
            rest = jnp.where(inside, 0.0, rest) - change
            parts[j + 2 :] = [rest[i : i + SUB] for i in range(0, rest.shape[0], SUB)]
    return jnp.concatenate(done, axis=0)


def factor(first, lower, second):
    n = first.shape[0]
    r = lax.broadcasted_iota(jnp.int32, (n, n), 0)
    c = lax.broadcasted_iota(jnp.int32, (n, n), 1)
    scales = []
    for block in (first, second):
        diag = jnp.where(r == c, block, 0.0)
        scales.append([lax.rsqrt(jnp.sum(diag, axis=i, keepdims=True)) for i in (0, 1)])
    (across1, down1), (across2, down2) = scales
    inv1 = block_inverse(jnp.where(r == c, 1.0, first * across1 * down1))
    lower = dot(lower * across1 * down2, inv1, HIGHEST, (1, 1))
    second = jnp.where(r == c, 1.0, second * across2 * down2)
    inv2 = block_inverse(second - dot(lower, lower, HIGHEST, (1, 1)))
    return across1, across2, inv1, lower, inv2


def inverse_factor(gram):
    half = gram.shape[0] // 2
    across1, across2, inv1, lower, inv2 = factor(gram[:half, :half], gram[half:, :half], gram[half:, half:])
    corner = -dot(inv2, dot(lower, inv1, HIGHEST), HIGHEST)
    left = jnp.concatenate([inv1, corner], axis=0) * across1
    right = jnp.concatenate([jnp.zeros_like(inv2), inv2], axis=0) * across2
    return jnp.concatenate([left, right], axis=1)


def whiten(x, *blocks):
    across1, across2, inv1, lower, inv2 = factor(*blocks)
    half = inv1.shape[0]
    left = dot(x[:, :half] * across1, inv1, HIGHEST, (1, 1))
    right = x[:, half:] * across2 - dot(left, lower, HIGHEST, (1, 1))
    return jnp.concatenate([left, dot(right, inv2, HIGHEST, (1, 1))], axis=1)


def square(n):
    return lax.broadcasted_iota(jnp.int32, (n, n), 0), lax.broadcasted_iota(jnp.int32, (n, n), 1)


def pick(core_ref, first, second):
    return jnp.where(core_ref[0] == 0, first, second)


def split_cores(core_ref, product, chips):
    share = product.shape[0] // (2 * chips)
    product = product.reshape(chips, 2, share, product.shape[1])
    even, odd = product[:, 0], product[:, 1]
    return pick(core_ref, even, odd), pick(core_ref, odd, even)


def sketch_kernel(rows_ref, cols_ref, core_ref, values_ref, test_ref, tile_ref, keep_ref, send_ref):
    count, width = values_ref.shape[0], values_ref.shape[1]
    tile_ref[...] = jnp.zeros_like(tile_ref)
    for n in range(count):
        row = pl.multiple_of(rows_ref[n] * width, width)
        col = pl.multiple_of(cols_ref[n] * width, width)
        tile_ref[pl.ds(row, width), pl.ds(col, width)] = values_ref[n]
    product = dot(tile_ref[...], test_ref[...])
    keep_ref[...], send_ref[...] = split_cores(core_ref, product, keep_ref.shape[0])


def cosketch_kernel(core_ref, tile_ref, sketch_ref, out_ref):
    sketch = sketch_ref[...]
    groups, _, half = out_ref.shape
    co = dot_terms(tile_ref[...], sketch, (0, 0))
    split = co.shape[0] // groups
    out_ref[:, :split, :] = co[:, :half].reshape(groups, split, half)
    out_ref[:, split : 2 * split, :] = co[:, half:].reshape(groups, split, half)
    chosen = pick(core_ref, sketch[:, :half], sketch[:, half:])
    gram = dot(sketch, chosen, HIGHEST, (0, 0))
    out_ref[:, 2 * split :, :] = gram.reshape(groups, gram.shape[0] // groups, half)


def resketch_kernel(core_ref, tile_ref, both_ref, keep_ref, send_ref, gram_ref):
    both = both_ref[...]
    side = tile_ref.shape[0]
    chips, share, rank = keep_ref.shape
    half = rank // 2
    split = side // both.shape[0]
    left = both[:, :split, :].reshape(side, half)
    right = both[:, split : 2 * split, :].reshape(side, half)
    product = dot_terms(tile_ref[...], jnp.concatenate([left, right], axis=1))
    keep_ref[...], send_ref[:, :share, :] = split_cores(core_ref, product, chips)
    gram = both[:, 2 * split :, :].reshape(rank, half)
    gram_ref[...] = gram
    wide = jnp.concatenate([gram[:half], gram[half:]], axis=1)
    send_ref[:, share:, :] = wide.reshape(chips, half // chips, rank)


def factor_kernel(core_ref, own_ref, received_ref, out_ref):
    rank, half = own_ref.shape
    share = received_ref.shape[1] - half // received_ref.shape[0]
    wide = received_ref[:, share:, :].reshape(half, rank)
    own, other = own_ref[...], jnp.concatenate([wide[:, :half], wide[:, half:]], axis=0)
    gram = jnp.concatenate([pick(core_ref, own, other), pick(core_ref, other, own)], axis=1)
    out_ref[...] = inverse_factor(gram)


def gram_kernel(parts_ref, inverse_ref, share_ref, gram_ref):
    share = dot(jnp.sum(parts_ref[...], axis=0), inverse_ref[...], HIGHEST, (1, 1))
    share_ref[...] = share
    gram = dot(share, share, HIGHEST, (0, 0))
    half = gram.shape[0] // 2
    r, c = square(half)
    last = gram[half:, half:]
    gram_ref[:half, :] = jnp.where(r >= c, gram[:half, :half], last)
    gram_ref[half : 2 * half, :] = gram[half:, :half]
    diag = jnp.sum(jnp.where(r == c, last, 0.0), axis=0, keepdims=True)
    spare = gram_ref.shape[0] - 2 * half
    gram_ref[2 * half :, :] = jnp.broadcast_to(diag, (spare, half))


def final_kernel(scale, share_ref, gram_ref, out_ref):
    gram = gram_ref[...]
    half = gram.shape[1]
    r, c = square(half)
    packed, lower = gram[:half], gram[half : 2 * half]
    mirror = packed.T
    first = jnp.where(r >= c, packed, mirror)
    second = jnp.where(r == c, gram[2 * half : 2 * half + 1], jnp.where(r < c, packed, mirror))
    out_ref[...] = whiten(share_ref[...], first, lower, second) * scale


FEAT = ("y", "core")


def to_each(x, axis):
    return lax.all_to_all(x, axis, 0, 0, tiled=True)


def from_each(x, axis):
    size = lax.axis_size(axis)
    return to_each(jnp.broadcast_to(x[None], (size,) + x.shape), axis)


def swap_cores(x):
    return lax.ppermute(x, "core", [(0, 1), (1, 0)])


def f32(*shape):
    return jax.ShapeDtypeStruct(shape, jnp.float32)


def per_device(block_values, block_rows, block_cols, test_matrix):
    values = block_values[0, 0]
    side, rank = test_matrix.shape
    half = rank // 2
    n_rows, chips = lax.axis_size("rows"), lax.axis_size("y")
    scale = float(side * n_rows) ** 0.5
    share = side // (2 * chips)
    core = lax.axis_index("core").astype(jnp.int32).reshape(1)

    tile, keep, send = pl.pallas_call(
        sketch_kernel,
        in_specs=[SMEM, SMEM, SMEM, VMEM, VMEM],
        out_specs=[VMEM] * 3,
        out_shape=[jax.ShapeDtypeStruct((side, side), jnp.bfloat16)] + [f32(chips, share, rank)] * 2,
        compiler_params=LARGE,
    )(block_rows[0, 0], block_cols[0, 0], core, values, test_matrix)
    sketch = jnp.sum(to_each(keep + swap_cores(send), "y"), axis=0)
    sketch = lax.all_gather(sketch, FEAT, axis=0, tiled=True)

    both = pl.pallas_call(
        cosketch_kernel,
        in_specs=[SMEM, VMEM, VMEM],
        out_specs=VMEM,
        out_shape=f32(n_rows, 2 * side // n_rows + rank // n_rows, half),
        compiler_params=PARAMS,
    )(core, tile, sketch)
    both = from_each(jnp.sum(to_each(both, "rows"), axis=0), "rows")

    keep, send, own = pl.pallas_call(
        resketch_kernel,
        in_specs=[SMEM, VMEM, VMEM],
        out_specs=[VMEM] * 3,
        out_shape=[f32(chips, share, rank), f32(chips, share + half // chips, rank), f32(rank, half)],
        compiler_params=PARAMS,
    )(core, tile, both)
    received = swap_cores(send)
    parts = to_each(keep + received[:, :share], "y")
    inverse = pl.pallas_call(
        factor_kernel,
        in_specs=[SMEM, VMEM, VMEM],
        out_specs=VMEM,
        out_shape=f32(rank, rank),
        compiler_params=PARAMS,
        cost_estimate=pl.CostEstimate(flops=10**10, bytes_accessed=10**6, transcendentals=0),
    )(core, own, received)

    resketch, gram = pl.pallas_call(
        gram_kernel,
        in_specs=[VMEM] * 2,
        out_specs=[VMEM] * 2,
        out_shape=[f32(share, rank), f32(rank + n_rows, half)],
        compiler_params=PARAMS,
    )(parts, inverse)
    gram = gram.reshape(n_rows, rank // n_rows + 1, 1, half)
    gram = jnp.sum(to_each(gram, "rows"), axis=0)
    gram = jnp.sum(from_each(gram, FEAT), axis=0)
    return pl.pallas_call(
        lambda *refs: final_kernel(scale, *refs),
        in_specs=[VMEM] * 2,
        out_specs=VMEM,
        out_shape=f32(share, rank),
        compiler_params=PARAMS,
    )(resketch, from_each(gram, "rows").reshape(rank + n_rows, half))


def solution(mesh):
    n_rows, n_feat = mesh.devices.shape
    chips = Mesh(mesh.devices.reshape(n_rows, n_feat // 2, 2), ("rows",) + FEAT)
    placed = (
        P("rows", FEAT, None, None, None),
        P("rows", FEAT, None),
        P("rows", FEAT, None),
        P(FEAT, None),
    )
    return jax.shard_map(
        per_device, mesh=chips, in_specs=placed, out_specs=P(("rows",) + FEAT, None), check_vma=False
    )
```
